512 devices in a mesh: seq: 64 (over y, z_hi, core), res: 8 (over z_lo, x).
Axes of the slice: x: 4, y: 8, z: 8 (z_hi: 4, z_lo: 2; z = z_hi * 2 + z_lo), core: 2. Of those that a mesh axis runs over, the one named last changes fastest.
Arguments:
- alignment_embedding: float32 [64, 1024, 256], P('seq', 'res'), may hold values from -2 to 2
- residue_couple_embedding: float32 [1024, 1024, 128], P('seq', 'res'), may hold values from -6 to 6
- couple_offset_matrix: float32 [128, 8], replicated, may hold values from -0.5 to 0.5
- horizontal_asker_matrix: bfloat16 [256, 256], replicated, may hold values from -24 to 24
- horizontal_lookup_matrix: bfloat16 [256, 256], replicated, may hold values from -24 to 24
- horizontal_content_matrix: bfloat16 [256, 256], replicated, may hold values from -0.375 to 0.375
- horizontal_sigmoid_matrix: bfloat16 [256, 256], replicated, may hold values from -0.375 to 0.375
- horizontal_final_matrix: bfloat16 [256, 256], replicated, may hold values from -1 to 1
- vertical_asker_matrix: bfloat16 [256, 256], replicated, may hold values from -24 to 24
- vertical_lookup_matrix: bfloat16 [256, 256], replicated, may hold values from -24 to 24
- vertical_content_matrix: bfloat16 [256, 256], replicated, may hold values from -0.375 to 0.375
- vertical_sigmoid_matrix: bfloat16 [256, 256], replicated, may hold values from -0.375 to 0.375
- vertical_final_matrix: bfloat16 [256, 256], replicated, may hold values from -1 to 1
Outputs:
- msa_out: float32 [64, 1024, 256], P('seq', 'res')
The draws below stay inside these ranges and needn't reach their ends.
All inputs are finite; a program needn't handle non-finite values.
Results may differ from the reference program's by a relative error of at most 0.023.
Values may be sent and summed in bfloat16 or wider, within the bound.
No kernel may reach another device: no remote copies, remote signals or barrier semaphores. Data moves between devices by JAX's collectives and lax.ppermute only.
A program may use at most 64 MiB of HBM per device.

```python
import jax
import jax.numpy as jnp
from jax import lax

ALIGN_FEATURES = 256
CZ = 128
HEADS = 8
SUBSPACE_WIDTH = 32
ALIGN_HOMOLOGS = 64
WINDOW_AMINOS = 1024


def base_matrix(key):
    return jax.random.truncated_normal(key, -4.0, 4.0, (ALIGN_FEATURES, ALIGN_FEATURES), jnp.float32) / jnp.sqrt(jnp.float32(ALIGN_FEATURES))


def draw_horizontal_lookup_matrix(key, part):
    base = base_matrix(jax.random.fold_in(key, 100))
    return base.astype(jnp.bfloat16)


def draw_horizontal_asker_matrix(key, part):
    key = jax.random.fold_in(key, 1)
    fresh_key = jax.random.fold_in(key, 0)
    weight = base_matrix(fresh_key)
    return weight.astype(jnp.bfloat16)


def draw_vertical_lookup_matrix(key, part):
    base = base_matrix(jax.random.fold_in(key, 200))
    return base.astype(jnp.bfloat16)


def draw_vertical_asker_matrix(key, part):
    key = jax.random.fold_in(key, 2)
    fresh_key = jax.random.fold_in(key, 0)
    weight = base_matrix(fresh_key)
    return weight.astype(jnp.bfloat16)


def block_levels(rng, extent, cuts, least, high):
    loudness = 1.0
    for axis_at, shards_of in cuts:
        steps = jax.random.uniform(jax.random.fold_in(jax.random.fold_in(rng, 6), axis_at), (shards_of,), jnp.float32, least / len(cuts), high / len(cuts))
        loudness = loudness * jnp.repeat(jnp.exp(steps), extent[axis_at] // shards_of).reshape((-1,) + (1,) * (len(extent) - 1 - axis_at))
    return loudness


def gaussian(own_key, extent, deviation, reach, pieces=(), dtype=jnp.bfloat16):
    loudness = block_levels(own_key, extent, pieces, -0.22, 0.18) if pieces else 1.0
    entries = jax.random.normal(own_key, extent, jnp.float32) * deviation * loudness
    return jnp.minimum(jnp.maximum(entries, -reach), reach).astype(dtype)


def setup_inputs(seed: int = 0) -> dict:
    key_of = jax.random.split(jax.random.key(seed), 14)
    return {
        "alignment_embedding": gaussian(key_of[0], (ALIGN_HOMOLOGS, WINDOW_AMINOS, ALIGN_FEATURES), 0.3, 2.0, ((0, 64), (1, 8)), jnp.float32),
        "residue_couple_embedding": gaussian(key_of[1], (WINDOW_AMINOS, WINDOW_AMINOS, CZ), 1.0, 6.0, ((0, 64), (1, 8)), jnp.float32),
        "couple_offset_matrix": gaussian(key_of[2], (CZ, HEADS), CZ ** -0.5, 0.5, (), jnp.float32),
        "horizontal_asker_matrix": draw_horizontal_asker_matrix(jax.random.fold_in(key_of[13], 71), 0),
        "horizontal_lookup_matrix": draw_horizontal_lookup_matrix(jax.random.fold_in(key_of[13], 71), 0),
        "horizontal_content_matrix": gaussian(key_of[5], (ALIGN_FEATURES, ALIGN_FEATURES), ALIGN_FEATURES ** -0.5, 0.375),
        "horizontal_sigmoid_matrix": gaussian(key_of[6], (ALIGN_FEATURES, ALIGN_FEATURES), ALIGN_FEATURES ** -0.5, 0.375),
        "horizontal_final_matrix": gaussian(key_of[7], (ALIGN_FEATURES, ALIGN_FEATURES), SUBSPACE_WIDTH ** -0.5, 1.0),
        "vertical_asker_matrix": draw_vertical_asker_matrix(jax.random.fold_in(key_of[13], 71), 0),
        "vertical_lookup_matrix": draw_vertical_lookup_matrix(jax.random.fold_in(key_of[13], 71), 0),
        "vertical_content_matrix": gaussian(key_of[10], (ALIGN_FEATURES, ALIGN_FEATURES), ALIGN_FEATURES ** -0.5, 0.375),
        "vertical_sigmoid_matrix": gaussian(key_of[11], (ALIGN_FEATURES, ALIGN_FEATURES), ALIGN_FEATURES ** -0.5, 0.375),
        "vertical_final_matrix": gaussian(key_of[12], (ALIGN_FEATURES, ALIGN_FEATURES), SUBSPACE_WIDTH ** -0.5, 1.0),
    }


EPS = 1e-05

def standardize_features(inputs):
    centre = lax.optimization_barrier(jnp.mean(inputs, axis=-1, keepdims=True))
    spread = lax.optimization_barrier(jnp.mean(jnp.square(inputs - centre), axis=-1, keepdims=True))
    return (inputs - centre) * lax.rsqrt(spread + EPS)

def attend(tokens, w_query, w_key, w_value, w_gate, w_out, extra):
    length = tokens.shape[0]
    standardized_source = standardize_features(tokens).astype(jnp.bfloat16)
    queries = jnp.dot(standardized_source, w_query, preferred_element_type=jnp.float32).astype(jnp.bfloat16).reshape(length, HEADS, SUBSPACE_WIDTH)
    key_rows = jnp.dot(standardized_source, w_key, preferred_element_type=jnp.float32).astype(jnp.bfloat16).reshape(length, HEADS, SUBSPACE_WIDTH)
    value_rows = jnp.dot(standardized_source, w_value, preferred_element_type=jnp.float32).astype(jnp.bfloat16).reshape(length, HEADS, SUBSPACE_WIDTH)
    gating = jax.nn.sigmoid(jnp.dot(standardized_source, w_gate, preferred_element_type=jnp.float32))
    logits = jnp.einsum('qhd,khd->hqk', queries.astype(jnp.float32), key_rows.astype(jnp.float32), precision=lax.Precision.HIGHEST) * SUBSPACE_WIDTH ** (-0.5) + extra
    row_max = lax.optimization_barrier(jnp.max(logits, axis=-1, keepdims=True))
    exponents = jnp.exp(logits - row_max)
    denominator = lax.optimization_barrier(jnp.sum(exponents, axis=-1))
    rounded = lax.optimization_barrier(exponents.astype(jnp.bfloat16))
    attended = jnp.einsum('hqk,khd->qhd', rounded.astype(jnp.float32), value_rows.astype(jnp.float32), precision=lax.Precision.HIGHEST)
    attended = attended / jnp.transpose(denominator)[:, :, None]
    gated_rows = (gating * attended.reshape(length, HEADS * SUBSPACE_WIDTH)).astype(jnp.bfloat16)
    return jnp.dot(gated_rows, w_out, preferred_element_type=jnp.float32)

def reference(alignment_embedding, residue_couple_embedding, couple_offset_matrix, horizontal_asker_matrix, horizontal_lookup_matrix, horizontal_content_matrix, horizontal_sigmoid_matrix, horizontal_final_matrix, vertical_asker_matrix, vertical_lookup_matrix, vertical_content_matrix, vertical_sigmoid_matrix, vertical_final_matrix):
    projected = jnp.einsum('ijc,ch->hij', standardize_features(residue_couple_embedding), couple_offset_matrix, precision=lax.Precision.HIGHEST)
    pair_bias = lax.optimization_barrier(projected.astype(jnp.bfloat16)).astype(jnp.float32)

    def horizontal_mixing_step(sequence):
        return sequence + attend(sequence, horizontal_asker_matrix, horizontal_lookup_matrix, horizontal_content_matrix, horizontal_sigmoid_matrix, horizontal_final_matrix, pair_bias)
    alignment_midway = lax.map(horizontal_mixing_step, alignment_embedding)

    def vertical_phase(residue):
        return residue + attend(residue, vertical_asker_matrix, vertical_lookup_matrix, vertical_content_matrix, vertical_sigmoid_matrix, vertical_final_matrix, jnp.float32(0.0))
    transposed_tensor = lax.map(vertical_phase, jnp.swapaxes(alignment_midway, 0, 1))
    return jnp.swapaxes(transposed_tensor, 0, 1)
```

```python
import functools

import jax
import jax.numpy as jnp
from jax import lax
from jax.experimental import pallas as pl
from jax.experimental.pallas import tpu as pltpu
from jax.sharding import Mesh, PartitionSpec as P

EPS = 1e-05
HEADS = 8
HEAD_SIZE = 32
FEATURES = HEADS * HEAD_SIZE
SCALE = HEAD_SIZE ** (-0.5)
Y, ZH, C, ZL, X = 8, 4, 2, 2, 4
SEQ = ("y", "zh", "c")
RES = ("zl", "x")
CHIPS = Y * ZH
VMEM = pl.BlockSpec(memory_space=pltpu.VMEM)
SMEM = pl.BlockSpec(memory_space=pltpu.SMEM)
NT = (((1,), (1,)), ((), ()))
F32, BF16 = jnp.float32, jnp.bfloat16


def call(kernel, out_shape, *args, scratch=(), smem=0, flops=0, size=0, vmem=48):
    return pl.pallas_call(
        kernel,
        out_shape=out_shape,
        in_specs=[SMEM] * smem + [VMEM] * (len(args) - smem),
        out_specs=jax.tree.map(lambda _: VMEM, out_shape),
        scratch_shapes=list(scratch),
        compiler_params=pltpu.CompilerParams(vmem_limit_bytes=vmem * 2**20),
        cost_estimate=pl.CostEstimate(flops=flops, bytes_accessed=size, transcendentals=0),
    )(*args)


def standardize(rows):
    centre = jnp.mean(rows, axis=-1, keepdims=True)
    moved = rows - centre
    spread = jnp.mean(moved * moved, axis=-1, keepdims=True)
    return moved * lax.rsqrt(spread + EPS)


def matmul(a, b):
    return jnp.dot(a, b, preferred_element_type=F32)


def head_mask(shape, head):
    lane = lax.broadcasted_iota(jnp.int32, shape, 1)
    return (lane >= head * HEAD_SIZE) & (lane < (head + 1) * HEAD_SIZE)


def pair_kernel(x_ref, w_ref, out_ref, scr):
    w = w_ref[...]
    wh = w.astype(BF16)
    wl = (w - wh.astype(F32)).astype(BF16)
    top = jnp.concatenate([wh.astype(F32), wh.astype(F32)], axis=1)
    low = jnp.concatenate([wl.astype(F32), jnp.zeros_like(w)], axis=1)
    weights = jnp.concatenate([top, low], axis=0).astype(BF16)
    for i in range(x_ref.shape[0]):
        d = standardize(x_ref[i])
        dh = d.astype(BF16)
        dl = (d - dh.astype(F32)).astype(BF16)
        both = jnp.concatenate([dh, dl], axis=1)
        part = lax.dot_general(weights, both, NT, preferred_element_type=F32)
        scr[:, i, :] = part[:HEADS] + part[HEADS:]
    out_ref[...] = scr[...].astype(BF16)


def norm_kernel(x_ref, out_ref):
    block = standardize(x_ref[...]).astype(BF16)
    for i in range(out_ref.shape[0]):
        out_ref[i] = block


def project_kernel(own_ref, pair_ref, rows_ref, wq_ref, wk_ref, wv_ref, wg_ref, q_ref, k_ref, v_ref, g_ref):
    for s, ref in enumerate((own_ref, pair_ref)):
        tokens = ref[...]
        k_ref[s] = matmul(tokens, wk_ref[...]).astype(BF16)
        v_ref[s] = matmul(tokens, wv_ref[...]).astype(BF16)
    count = rows_ref.shape[1]
    tokens = standardize(rows_ref[...].reshape(2 * count, FEATURES)).astype(BF16)
    g_ref[...] = jax.nn.sigmoid(matmul(tokens, wg_ref[...])).reshape(2, count, FEATURES)
    q = matmul(tokens, wq_ref[...])
    for h in range(HEADS):
        masked = jnp.where(head_mask(q.shape, h), q, 0.0).astype(BF16)
        q_ref[:, h * count : (h + 1) * count, :] = masked.reshape(2, count, FEATURES)


def row_kernel(c_ref, bias_ref, q_ref, k_ref, v_ref, g_ref, rows_ref, wo_ref, mid_ref, send_ref, s_scr, p_scr, t_scr):
    count = rows_ref.shape[1]
    keys = k_ref.shape[1]
    cols = keys // Y
    gated = []
    for s in range(2):
        s_scr[s] = lax.dot_general(q_ref[s], k_ref[s], NT, preferred_element_type=F32)
    for s in range(2):
        sums = []
        for h in range(HEADS):
            lo, hi = h * count, (h + 1) * count
            logits = []
            for y in range(Y):
                bias = bias_ref[y * ZH : (y + 1) * ZH, h].astype(F32).reshape(count, cols)
                logits.append(s_scr[s, lo:hi, y * cols : (y + 1) * cols] * SCALE + bias)
            top = functools.reduce(jnp.maximum, logits)
            top = jnp.max(top, axis=-1, keepdims=True)
            total = None
            for y in range(Y):
                e = jnp.exp(logits[y] - top)
                total = e if total is None else total + e
                p_scr[s, lo:hi, y * cols : (y + 1) * cols] = e.astype(BF16)
            sums.append(jnp.sum(total, axis=-1, keepdims=True))
        out = matmul(p_scr[s], v_ref[s])
        attended = jnp.zeros((count, FEATURES), F32)
        for h in range(HEADS):
            attended = jnp.where(
                head_mask(attended.shape, h), out[h * count : (h + 1) * count] / sums[h], attended
            )
        gated.append((g_ref[s] * attended).astype(BF16))
    delta = matmul(jnp.concatenate(gated, axis=0), wo_ref[...])
    mids = [rows_ref[s] + delta[s * count : (s + 1) * count] for s in range(2)]
    normed = []
    for s in range(2):
        mid_ref[s] = mids[s]
        normed.append(standardize(mids[s]))
    first = c_ref[0] == 0
    ordered = [jnp.where(first, normed[0], normed[1]), jnp.where(first, normed[1], normed[0])]
    for s in range(2):
        for rr in range(2):
            for half in range(2):
                block = ordered[s][rr * CHIPS : (rr + 1) * CHIPS, half * 128 : (half + 1) * 128]
                t_scr[pl.ds(s * 4 + rr * 2 + half, CHIPS, stride=8), :] = block
    send_ref[...] = t_scr[...].reshape(CHIPS, 8, 128).astype(BF16)


def column_kernel(x_ref, wq_ref, wk_ref, wv_ref, wg_ref, out_ref, t_scr):
    t_scr[...] = x_ref[...].astype(F32).reshape(CHIPS * 8, 128)
    part = [t_scr[pl.ds(i, CHIPS, stride=8), :] for i in range(8)]
    count = 2 * CHIPS
    tokens = jnp.concatenate(
        [
            jnp.concatenate([part[s * 4 + rr * 2], part[s * 4 + rr * 2 + 1]], axis=1)
            for rr in range(2)
            for s in range(2)
        ],
        axis=0,
    ).astype(BF16)
    q = matmul(tokens, wq_ref[...])
    k = matmul(tokens, wk_ref[...]).astype(BF16)
    v = matmul(tokens, wv_ref[...]).astype(BF16)
    g = jax.nn.sigmoid(matmul(tokens, wg_ref[...]))
    for rr in range(2):
        lo, hi = rr * count, (rr + 1) * count
        masked = jnp.concatenate(
            [jnp.where(head_mask((count, FEATURES), h), q[lo:hi], 0.0) for h in range(HEADS)], axis=0
        ).astype(BF16)
        logits = lax.dot_general(masked, k[lo:hi], NT, preferred_element_type=F32) * SCALE
        e = jnp.exp(logits - jnp.max(logits, axis=-1, keepdims=True))
        total = jnp.sum(e, axis=-1, keepdims=True)
        out = matmul(e.astype(BF16), v[lo:hi]) / total
        attended = jnp.zeros((count, FEATURES), F32)
        for h in range(HEADS):
            attended = jnp.where(
                head_mask(attended.shape, h), out[h * count : (h + 1) * count], attended
            )
        gated = g[lo:hi] * attended
        for s in range(2):
            for half in range(2):
                t_scr[pl.ds(s * 4 + rr * 2 + half, CHIPS, stride=8), :] = gated[
                    s * CHIPS : (s + 1) * CHIPS, half * 128 : (half + 1) * 128
                ]
    out_ref[...] = t_scr[...].reshape(CHIPS, 8, 128).astype(BF16)


def final_kernel(c_ref, x_ref, own_ref, pair_ref, wo_ref, out_ref, t_scr):
    t_scr[...] = x_ref[...].astype(F32).reshape(CHIPS * 8, 128)
    part = [t_scr[pl.ds(i, CHIPS, stride=8), :] for i in range(8)]
    tokens = jnp.concatenate(
        [
            jnp.concatenate([part[s * 4 + rr * 2], part[s * 4 + rr * 2 + 1]], axis=1)
            for s in range(2)
            for rr in range(2)
        ],
        axis=0,
    ).astype(BF16)
    update = matmul(tokens, wo_ref[...])
    first = c_ref[0] == 0
    own, pair = own_ref[...], pair_ref[...]
    middle = [jnp.where(first, own, pair), jnp.where(first, pair, own)]
    count = own.shape[0]
    step = count // ZH
    for s in range(2):
        result = middle[s] + update[s * count : (s + 1) * count]
        for z in range(ZH):
            at = (z * 2 + s) * step
            out_ref[at : at + step] = result[z * step : (z + 1) * step]


def shards(
    alignment,
    pair,
    offset_matrix,
    row_wq,
    row_wk,
    row_wv,
    row_wg,
    row_wo,
    col_wq,
    col_wk,
    col_wv,
    col_wg,
    col_wo,
):
    core = lax.axis_index("c")
    core_ref = core.astype(jnp.int32).reshape(1)
    tokens = alignment.shape[1]
    half = tokens // 2
    swap = [(0, 1), (1, 0)]
    turn = [(a * 8 + b, b * 8 + a) for a in range(8) for b in range(8)]

    bias = call(
        pair_kernel,
        jax.ShapeDtypeStruct((HEADS, pair.shape[0], pair.shape[1]), BF16),
        pair,
        offset_matrix.T,
        scratch=[pltpu.VMEM((HEADS, pair.shape[0], pair.shape[1]), F32)],
    )
    bias = lax.ppermute(bias, ("y", "zl", "x"), turn)

    rows = alignment[0].reshape(ZH, 2, half // ZH, FEATURES)
    mine = jnp.where(core == 0, rows[:, 0], rows[:, 1]).reshape(half, FEATURES)
    other = jnp.where(core == 0, rows[:, 1], rows[:, 0]).reshape(half, FEATURES)
    other = lax.ppermute(other, "c", swap)
    query_rows = jnp.stack([mine, other])

    spread = call(
        norm_kernel, jax.ShapeDtypeStruct((8, tokens, FEATURES), BF16), alignment[0]
    )
    own_normed = lax.all_to_all(spread, RES, 0, 0, tiled=True).reshape(8 * tokens, FEATURES)
    pair_normed = lax.ppermute(own_normed, "c", swap)

    wide = jnp.broadcast_to(bias[None], (CHIPS,) + bias.shape)
    wide = lax.all_to_all(wide, ("y", "zh"), 0, 0, tiled=True)

    keys = 8 * tokens
    q, k, v, g = call(
        project_kernel,
        (
            jax.ShapeDtypeStruct((2, HEADS * half, FEATURES), BF16),
            jax.ShapeDtypeStruct((2, keys, FEATURES), BF16),
            jax.ShapeDtypeStruct((2, keys, FEATURES), BF16),
            jax.ShapeDtypeStruct((2, half, FEATURES), F32),
        ),
        own_normed,
        pair_normed,
        query_rows,
        row_wq,
        row_wk,
        row_wv,
        row_wg,
        flops=2 * 2 * keys * FEATURES * 2 * FEATURES,
        size=4 * 2**20,
    )
    middle, send = call(
        row_kernel,
        (
            jax.ShapeDtypeStruct((2, half, FEATURES), F32),
            jax.ShapeDtypeStruct((CHIPS, 8, 128), BF16),
        ),
        core_ref,
        wide,
        q,
        k,
        v,
        g,
        query_rows,
        row_wo,
        smem=1,
        scratch=[
            pltpu.VMEM((2, HEADS * half, keys), F32),
            pltpu.VMEM((2, HEADS * half, keys), BF16),
            pltpu.VMEM((CHIPS * 8, 128), F32),
        ],
        flops=2 * 2 * 2 * HEADS * half * keys * FEATURES,
        size=6 * 2**20,
    )
    middle_pair = lax.ppermute(middle[1], "c", swap)

    block = lax.all_to_all(send, ("y", "zh"), 0, 0, tiled=True)
    gated = call(
        column_kernel,
        jax.ShapeDtypeStruct((CHIPS, 8, 128), BF16),
        block,
        col_wq,
        col_wk,
        col_wv,
        col_wg,
        scratch=[pltpu.VMEM((CHIPS * 8, 128), F32)],
    )
    back = lax.all_to_all(gated.reshape(2 * CHIPS, 4, 128), SEQ, 0, 0, tiled=True)
    out = call(
        final_kernel,
        jax.ShapeDtypeStruct((tokens, FEATURES), F32),
        core_ref,
        back.reshape(CHIPS, 8, 128),
        middle[0],
        middle_pair,
        col_wo,
        smem=1,
        scratch=[pltpu.VMEM((CHIPS * 8, 128), F32)],
    )
    return out[None]


def solution(mesh):
    fine = Mesh(mesh.devices.reshape(Y, ZH, C, ZL, X), ("y", "zh", "c", "zl", "x"))
    split = P(SEQ, RES, None)
    in_specs = (split, split) + (P(),) * 11
    return jax.shard_map(shards, mesh=fine, in_specs=in_specs, out_specs=split, check_vma=False)
```

```python
import functools

import jax
import jax.numpy as jnp
from jax import lax
from jax.experimental import pallas as pl
from jax.experimental.pallas import tpu as pltpu
from jax.sharding import Mesh, PartitionSpec as P

EPS = 1e-05
HEADS = 8
HEAD_SIZE = 32
FEATURES = HEADS * HEAD_SIZE
SCALE = HEAD_SIZE ** (-0.5)
Y, ZH, C, ZL, X = 8, 4, 2, 2, 4
SEQ = ("y", "zh", "c")
RES = ("zl", "x")
CHIPS = Y * ZH
BLOCKS = ZL * X
TURN = (4, 3, 1, 5, 7, 2, 0, 6)
TURN_BITS = sum(y << (4 * n) for n, y in enumerate(TURN))
VMEM = pl.BlockSpec(memory_space=pltpu.VMEM)
SMEM = pl.BlockSpec(memory_space=pltpu.SMEM)
HBM = pl.BlockSpec(memory_space=pltpu.HBM)
NT = (((1,), (1,)), ((), ()))
F32, BF16 = jnp.float32, jnp.bfloat16


def call(kernel, out_shape, *args, scratch=(), smem=0, hbm=0, flops=0, size=0, vmem=6):
    vmem_count = len(args) - smem - hbm
    pinned = [pltpu.with_memory_space_constraint(x, pltpu.HBM) for x in args[len(args) - hbm :]]
    return pl.pallas_call(
        kernel,
        out_shape=out_shape,
        in_specs=[SMEM] * smem + [VMEM] * vmem_count + [HBM] * hbm,
        out_specs=jax.tree.map(lambda _: VMEM, out_shape),
        scratch_shapes=list(scratch),
        compiler_params=pltpu.CompilerParams(vmem_limit_bytes=vmem * 2**20),
        cost_estimate=pl.CostEstimate(flops=flops, bytes_accessed=size, transcendentals=0),
    )(*args[: len(args) - hbm], *pinned)


def standardize(rows):
    centre = jnp.mean(rows, axis=-1, keepdims=True)
    moved = rows - centre
    spread = jnp.mean(moved * moved, axis=-1, keepdims=True)
    return moved * lax.rsqrt(spread + EPS)


def matmul(a, b):
    return jnp.dot(a, b, preferred_element_type=F32)


def head_mask(shape, head):
    lane = lax.broadcasted_iota(jnp.int32, shape, 1)
    return (lane >= head * HEAD_SIZE) & (lane < (head + 1) * HEAD_SIZE)


def pair_kernel(w_hbm, x_ref, out_ref, w_ref, x_scr, scr, sems):
    count = x_ref.shape[0]
    parts = sems.shape[0] - 1
    step = count // parts
    first = pltpu.make_async_copy(w_hbm, w_ref, sems.at[parts])
    first.start()
    copies = []
    for n in range(parts):
        part = pl.ds(n * step, step)
        copies.append(pltpu.make_async_copy(x_ref.at[part], x_scr.at[part], sems.at[n]))
        copies[n].start()
    first.wait()
    w = w_ref[...]
    wh = w.astype(BF16)
    wl = (w - wh.astype(F32)).astype(BF16)
    top = jnp.concatenate([wh.astype(F32), wh.astype(F32)], axis=1)
    low = jnp.concatenate([wl.astype(F32), jnp.zeros_like(w)], axis=1)
    weights = jnp.concatenate([top, low], axis=0).astype(BF16)
    for i in range(count):
        if i % step == 0:
            copies[i // step].wait()
        d = standardize(x_scr[i])
        dh = d.astype(BF16)
        dl = (d - dh.astype(F32)).astype(BF16)
        both = jnp.concatenate([dh, dl], axis=1)
        part = lax.dot_general(weights, both, NT, preferred_element_type=F32)
        scr[:, i, :] = part[:HEADS] + part[HEADS:]
    out_ref[...] = scr[...].astype(BF16)


def norm_kernel(x_ref, out_ref):
    out_ref[...] = standardize(x_ref[...]).astype(BF16)


def query_kernel(c_ref, rows_ref, wq_ref, wg_ref, q_ref, g_ref, mine_ref):
    core = c_ref[0]
    mine = jnp.concatenate([rows_ref[core, :, core], rows_ref[1 - core, :, core]], axis=0)
    mine = mine.reshape(-1, FEATURES)
    mine_ref[...] = mine.reshape(mine_ref.shape)
    tokens = standardize(mine).astype(BF16)
    g_ref[...] = jax.nn.sigmoid(matmul(tokens, wg_ref[...])).reshape(g_ref.shape)
    q_ref[...] = matmul(tokens, wq_ref[...]).astype(BF16).reshape(q_ref.shape)


def row_kernel(
    c_ref, here_ref, q_ref, own_ref, pair_ref, wk_ref, wv_ref, bias_ref, g_ref, rows_ref, wo_ref,
    mid_ref, pair_mid_ref, send_ref, s_scr, p_scr, v_scr, t_scr
):
    count = rows_ref.shape[1]
    keys = own_ref.shape[0]
    cols = keys // BLOCKS
    here = here_ref[0]
    at = []
    for n in range(BLOCKS):
        block = (n % ZL) * X + n // ZL
        at.append((here ^ ((TURN_BITS >> (4 * (here ^ block))) & 7)) * ZH)
    gated, outs, sums = [], [], []

    def softmax(s):
        for h in range(HEADS):
            lo, hi = h * count, (h + 1) * count
            logits = []
            for n in range(BLOCKS):
                bias = bias_ref[pl.ds(at[n], ZH), h].astype(F32).reshape(count, cols)
                logits.append(s_scr[s, lo:hi, n * cols : (n + 1) * cols] * SCALE + bias)
            top = functools.reduce(jnp.maximum, logits)
            top = jnp.max(top, axis=-1, keepdims=True)
            total = None
            for n in range(BLOCKS):
                e = jnp.exp(logits[n] - top)
                total = e if total is None else total + e
                p_scr[s, lo:hi, n * cols : (n + 1) * cols] = e.astype(BF16)
            sums.append(jnp.sum(total, axis=-1, keepdims=True))

    for s, ref in enumerate((own_ref, pair_ref)):
        tokens = ref[...]
        k = matmul(tokens, wk_ref[...]).astype(BF16)
        v_scr[s] = matmul(tokens, wv_ref[...]).astype(BF16)
        q = q_ref[s].astype(F32)
        masked = [jnp.where(head_mask(q.shape, h), q, 0.0).astype(BF16) for h in range(HEADS)]
        masked = jnp.concatenate(masked, axis=0)
        s_scr[s] = lax.dot_general(masked, k, NT, preferred_element_type=F32)
    for s in range(2):
        softmax(s)
        outs.append(matmul(p_scr[s], v_scr[s]))
    for s in range(2):
        attended = jnp.zeros((count, FEATURES), F32)
        for h in range(HEADS):
            part = outs[s][h * count : (h + 1) * count] / sums[s * HEADS + h]
            attended = jnp.where(head_mask(attended.shape, h), part, attended)
        gated.append((g_ref[s] * attended).astype(BF16))
    delta = matmul(jnp.concatenate(gated, axis=0), wo_ref[...])
    mids = [rows_ref[s] + delta[s * count : (s + 1) * count] for s in range(2)]
    mid_ref[...] = mids[0]
    pair_mid_ref[...] = mids[1]
    normed = [standardize(mid) for mid in mids]
    first = c_ref[0] == 0
    ordered = [jnp.where(first, normed[0], normed[1]), jnp.where(first, normed[1], normed[0])]
    for s in range(2):
        for rr in range(2):
            for half in range(2):
                block = ordered[s][rr * CHIPS : (rr + 1) * CHIPS, half * 128 : (half + 1) * 128]
                t_scr[pl.ds(s * 4 + rr * 2 + half, CHIPS, stride=8), :] = block
    send_ref[...] = t_scr[...].reshape(CHIPS, 8, 128).astype(BF16)


def row_call(core_ref, here_ref, q, own, pair, wk, wv, wide, g, mine, wo):
    half, keys = mine.shape[1], own.shape[0]
    return call(
        row_kernel,
        (
            jax.ShapeDtypeStruct((half, FEATURES), F32),
            jax.ShapeDtypeStruct((half, FEATURES), F32),
            jax.ShapeDtypeStruct((CHIPS, 8, 128), BF16),
        ),
        core_ref,
        here_ref,
        q,
        own,
        pair,
        wk,
        wv,
        wide,
        g,
        mine,
        wo,
        smem=2,
        scratch=[
            pltpu.VMEM((2, HEADS * half, keys), F32),
            pltpu.VMEM((2, HEADS * half, keys), BF16),
            pltpu.VMEM((2, keys, FEATURES), BF16),
            pltpu.VMEM((CHIPS * 8, 128), F32),
        ],
        flops=2 * 2 * 2 * HEADS * half * keys * FEATURES,
        size=6 * 2**20,
        vmem=20,
    )


def column_kernel(x_ref, wq_ref, wk_ref, wv_ref, wg_ref, out_ref, t_scr):
    t_scr[...] = x_ref[...].astype(F32).reshape(CHIPS * 8, 128)
    part = [t_scr[pl.ds(i, CHIPS, stride=8), :] for i in range(8)]
    count = 2 * CHIPS
    tokens = jnp.concatenate(
        [
            jnp.concatenate([part[s * 4 + rr * 2], part[s * 4 + rr * 2 + 1]], axis=1)
            for rr in range(2)
            for s in range(2)
        ],
        axis=0,
    ).astype(BF16)
    q = matmul(tokens, wq_ref[...])
    k = matmul(tokens, wk_ref[...]).astype(BF16)
    v = matmul(tokens, wv_ref[...]).astype(BF16)
    g = jax.nn.sigmoid(matmul(tokens, wg_ref[...]))
    for rr in range(2):
        lo, hi = rr * count, (rr + 1) * count
        masked = jnp.concatenate(
            [jnp.where(head_mask((count, FEATURES), h), q[lo:hi], 0.0) for h in range(HEADS)], axis=0
        ).astype(BF16)
        logits = lax.dot_general(masked, k[lo:hi], NT, preferred_element_type=F32) * SCALE
        e = jnp.exp(logits - jnp.max(logits, axis=-1, keepdims=True))
        total = jnp.sum(e, axis=-1, keepdims=True)
        out = matmul(e.astype(BF16), v[lo:hi]) / total
        attended = jnp.zeros((count, FEATURES), F32)
        for h in range(HEADS):
            attended = jnp.where(
                head_mask(attended.shape, h), out[h * count : (h + 1) * count], attended
            )
        gated = g[lo:hi] * attended
        for s in range(2):
            for half in range(2):
                t_scr[pl.ds(s * 4 + rr * 2 + half, CHIPS, stride=8), :] = gated[
                    s * CHIPS : (s + 1) * CHIPS, half * 128 : (half + 1) * 128
                ]
    out_ref[...] = t_scr[...].reshape(CHIPS, 8, 128).astype(BF16)


def final_kernel(c_ref, x_ref, own_ref, pair_ref, wo_ref, out_ref, t_scr):
    t_scr[...] = x_ref[...].astype(F32).reshape(CHIPS * 8, 128)
    part = [t_scr[pl.ds(i, CHIPS, stride=8), :] for i in range(8)]
    tokens = jnp.concatenate(
        [
            jnp.concatenate([part[s * 4 + rr * 2], part[s * 4 + rr * 2 + 1]], axis=1)
            for s in range(2)
            for rr in range(2)
        ],
        axis=0,
    ).astype(BF16)
    update = matmul(tokens, wo_ref[...])
    first = c_ref[0] == 0
    own, pair = own_ref[...], pair_ref[...]
    middle = [jnp.where(first, own, pair), jnp.where(first, pair, own)]
    count = own.shape[0]
    step = count // ZH
    for s in range(2):
        result = middle[s] + update[s * count : (s + 1) * count]
        for z in range(ZH):
            at = (z * 2 + s) * step
            out_ref[at : at + step] = result[z * step : (z + 1) * step]


def shards(
    alignment,
    pair,
    offset_matrix,
    row_wq,
    row_wk,
    row_wv,
    row_wg,
    row_wo,
    col_wq,
    col_wk,
    col_wv,
    col_wg,
    col_wo,
):
    core = lax.axis_index("c").astype(jnp.int32)
    core_ref = core.reshape(1)
    tokens = alignment.shape[1]
    half = tokens // 2
    swap = [(0, 1), (1, 0)]
    turn = [
        (b * BLOCKS + r, (b ^ TURN[b ^ r]) * BLOCKS + b) for b in range(BLOCKS) for r in range(BLOCKS)
    ]

    pair_shape = pair.shape
    bias_shape = (HEADS, pair_shape[0], pair_shape[1])
    bias_here = call(
        pair_kernel,
        jax.ShapeDtypeStruct(bias_shape, BF16),
        offset_matrix.T,
        pair,
        hbm=2,
        scratch=[
            pltpu.VMEM((HEADS, pair_shape[2]), F32),
            pltpu.VMEM(pair_shape, F32),
            pltpu.VMEM(bias_shape, F32),
            pltpu.SemaphoreType.DMA((2,)),
        ],
    )
    bias = lax.ppermute(bias_here, ("y", "zl", "x"), turn)
    normed = call(norm_kernel, jax.ShapeDtypeStruct((tokens, FEATURES), BF16), alignment[0])
    near_normed = lax.all_gather(normed, "zl", axis=0, tiled=True)
    near_normed, bias = lax.optimization_barrier((near_normed, bias))
    own_normed = lax.all_gather(near_normed, "x", axis=0, tiled=True)
    pair_normed = lax.ppermute(own_normed, "c", swap)
    rows = lax.all_gather(alignment, "c", axis=0, tiled=True)
    rows = rows.reshape(2, ZH, 2, half // ZH, FEATURES)

    wide = jnp.broadcast_to(bias[None], (CHIPS,) + bias.shape)
    wide = lax.all_to_all(wide, ("y", "zh"), 0, 0, tiled=True)

    here_ref = lax.axis_index(RES).astype(jnp.int32).reshape(1)
    q, g, mine = call(
        query_kernel,
        (
            jax.ShapeDtypeStruct((2, half, FEATURES), BF16),
            jax.ShapeDtypeStruct((2, half, FEATURES), F32),
            jax.ShapeDtypeStruct((2, half, FEATURES), F32),
        ),
        core_ref,
        rows,
        row_wq,
        row_wg,
        smem=1,
        flops=2 * 2 * half * FEATURES * 2 * FEATURES,
        size=2**20,
    )
    middle, middle_pair, send = row_call(
        core_ref, here_ref, q, own_normed, pair_normed, row_wk, row_wv, wide, g, mine, row_wo
    )
    middle_pair = lax.ppermute(middle_pair, "c", swap)

    block = lax.all_to_all(send, ("y", "zh"), 0, 0, tiled=True)
    gated = call(
        column_kernel,
        jax.ShapeDtypeStruct((CHIPS, 8, 128), BF16),
        block,
        col_wq,
        col_wk,
        col_wv,
        col_wg,
        scratch=[pltpu.VMEM((CHIPS * 8, 128), F32)],
    )
    back = lax.all_to_all(gated.reshape(2 * CHIPS, 4, 128), SEQ, 0, 0, tiled=True)
    out = call(
        final_kernel,
        jax.ShapeDtypeStruct((tokens, FEATURES), F32),
        core_ref,
        back.reshape(CHIPS, 8, 128),
        middle,
        middle_pair,
        col_wo,
        smem=1,
        scratch=[pltpu.VMEM((CHIPS * 8, 128), F32)],
    )
    return out[None]


def solution(mesh):
    fine = Mesh(mesh.devices.reshape(Y, ZH, C, ZL, X), ("y", "zh", "c", "zl", "x"))
    split = P(SEQ, RES, None)
    in_specs = (split, split) + (P(),) * 11
    return jax.shard_map(shards, mesh=fine, in_specs=in_specs, out_specs=split, check_vma=False)
```

```python
import functools

import jax
import jax.numpy as jnp
from jax import lax
from jax.experimental import pallas as pl
from jax.experimental.pallas import tpu as pltpu
from jax.sharding import Mesh, PartitionSpec as P

EPS = 1e-05
HEADS = 8
HEAD_SIZE = 32
FEATURES = HEADS * HEAD_SIZE
SCALE = HEAD_SIZE ** (-0.5)
Y, ZH, C, ZL, X = 8, 4, 2, 2, 4
SEQ = ("y", "zh", "c")
RES = ("zl", "x")
CHIPS = Y * ZH
BLOCKS = ZL * X
TURN = (4, 3, 1, 5, 7, 2, 0, 6)
TURN_BITS = sum(y << (4 * n) for n, y in enumerate(TURN))
VMEM = pl.BlockSpec(memory_space=pltpu.VMEM)
SMEM = pl.BlockSpec(memory_space=pltpu.SMEM)
HBM = pl.BlockSpec(memory_space=pltpu.HBM)
NT = (((1,), (1,)), ((), ()))
F32, BF16 = jnp.float32, jnp.bfloat16


def call(kernel, out_shape, *args, scratch=(), smem=0, hbm=0, flops=0, size=0, vmem=6):
    vmem_count = len(args) - smem - hbm
    pinned = [pltpu.with_memory_space_constraint(x, pltpu.HBM) for x in args[len(args) - hbm :]]
    return pl.pallas_call(
        kernel,
        out_shape=out_shape,
        in_specs=[SMEM] * smem + [VMEM] * vmem_count + [HBM] * hbm,
        out_specs=jax.tree.map(lambda _: VMEM, out_shape),
        scratch_shapes=list(scratch),
        compiler_params=pltpu.CompilerParams(vmem_limit_bytes=vmem * 2**20),
        cost_estimate=pl.CostEstimate(flops=flops, bytes_accessed=size, transcendentals=0),
    )(*args[: len(args) - hbm], *pinned)


def standardize(rows):
    centre = jnp.mean(rows, axis=-1, keepdims=True)
    moved = rows - centre
    spread = jnp.mean(moved * moved, axis=-1, keepdims=True)
    return moved * lax.rsqrt(spread + EPS)


def matmul(a, b):
    return jnp.dot(a, b, preferred_element_type=F32)


def head_mask(shape, head):
    lane = lax.broadcasted_iota(jnp.int32, shape, 1)
    return (lane >= head * HEAD_SIZE) & (lane < (head + 1) * HEAD_SIZE)


def pair_kernel(w_hbm, x_ref, out_ref, w_ref, x_scr, scr, sems):
    count = x_ref.shape[0]
    parts = sems.shape[0] - 1
    step = count // parts
    first = pltpu.make_async_copy(w_hbm, w_ref, sems.at[parts])
    first.start()
    copies = []
    for n in range(parts):
        part = pl.ds(n * step, step)
        copies.append(pltpu.make_async_copy(x_ref.at[part], x_scr.at[part], sems.at[n]))
        copies[n].start()
    first.wait()
    w = w_ref[...]
    wh = w.astype(BF16)
    wl = (w - wh.astype(F32)).astype(BF16)
    top = jnp.concatenate([wh.astype(F32), wh.astype(F32)], axis=1)
    low = jnp.concatenate([wl.astype(F32), jnp.zeros_like(w)], axis=1)
    weights = jnp.concatenate([top, low], axis=0).astype(BF16)
    for i in range(count):
        if i % step == 0:
            copies[i // step].wait()
        d = standardize(x_scr[i])
        dh = d.astype(BF16)
        dl = (d - dh.astype(F32)).astype(BF16)
        both = jnp.concatenate([dh, dl], axis=1)
        part = lax.dot_general(weights, both, NT, preferred_element_type=F32)
        scr[:, i, :] = part[:HEADS] + part[HEADS:]
    out_ref[...] = scr[...].astype(BF16)


def norm_kernel(x_ref, out_ref):
    out_ref[...] = standardize(x_ref[...]).astype(BF16)


def query_kernel(c_ref, rows_ref, wq_ref, wg_ref, q_ref, g_ref, mine_ref):
    core = c_ref[0]
    mine = jnp.concatenate([rows_ref[core, :, core], rows_ref[1 - core, :, core]], axis=0)
    mine = mine.reshape(-1, FEATURES)
    mine_ref[...] = mine.reshape(mine_ref.shape)
    tokens = standardize(mine).astype(BF16)
    g_ref[...] = jax.nn.sigmoid(matmul(tokens, wg_ref[...])).reshape(g_ref.shape)
    q_ref[...] = matmul(tokens, wq_ref[...]).astype(BF16).reshape(q_ref.shape)


def row_kernel(
    c_ref, here_ref, q_ref, own_ref, pair_ref, wk_ref, wv_ref, bias_ref, g_ref, rows_ref, wo_ref,
    send_ref, s_scr, p_scr, v_scr, t_scr
):
    count = rows_ref.shape[1]
    keys = own_ref.shape[0]
    cols = keys // BLOCKS
    here = here_ref[0]
    at = []
    for n in range(BLOCKS):
        block = (n % ZL) * X + n // ZL
        at.append((here ^ ((TURN_BITS >> (4 * (here ^ block))) & 7)) * ZH)
    gated, outs, shares = [], [], []

    def softmax(s):
        for h in range(HEADS):
            lo, hi = h * count, (h + 1) * count
            logits = []
            for n in range(BLOCKS):
                bias = bias_ref[pl.ds(at[n], ZH), h].astype(F32).reshape(count, cols)
                logits.append(s_scr[s, lo:hi, n * cols : (n + 1) * cols] * SCALE + bias)
            top = functools.reduce(jnp.maximum, logits)
            top = jnp.max(top, axis=-1, keepdims=True)
            total = None
            for n in range(BLOCKS):
                e = jnp.exp(logits[n] - top)
                total = e if total is None else total + e
                p_scr[s, lo:hi, n * cols : (n + 1) * cols] = e.astype(BF16)
            shares.append(1.0 / jnp.sum(total, axis=-1, keepdims=True))

    for s, ref in enumerate((own_ref, pair_ref)):
        tokens = ref[...]
        k = matmul(tokens, wk_ref[...]).astype(BF16)
        v_scr[s] = matmul(tokens, wv_ref[...]).astype(BF16)
        q = q_ref[s].astype(F32)
        masked = [jnp.where(head_mask(q.shape, h), q, 0.0).astype(BF16) for h in range(HEADS)]
        masked = jnp.concatenate(masked, axis=0)
        s_scr[s] = lax.dot_general(masked, k, NT, preferred_element_type=F32)
    for s in range(2):
        softmax(s)
        outs.append(matmul(p_scr[s], v_scr[s]))
    for s in range(2):
        attended = jnp.zeros((count, FEATURES), F32)
        for h in range(HEADS):
            part = outs[s][h * count : (h + 1) * count] * shares[s * HEADS + h]
            attended = jnp.where(head_mask(attended.shape, h), part, attended)
        gated.append((g_ref[s] * attended).astype(BF16))
    delta = matmul(jnp.concatenate(gated, axis=0), wo_ref[...])
    first = c_ref[0] == 0
    deltas = [delta[s * count : (s + 1) * count] for s in range(2)]
    normed = [standardize(rows_ref[s] + deltas[s]) for s in range(2)]
    for kind, (own, pair) in enumerate((normed, deltas)):
        ordered = [jnp.where(first, own, pair), jnp.where(first, pair, own)]
        for s in range(2):
            for rr in range(2):
                for half in range(2):
                    block = ordered[s][rr * CHIPS : (rr + 1) * CHIPS, half * 128 : (half + 1) * 128]
                    t_scr[pl.ds(kind * 8 + s * 4 + rr * 2 + half, CHIPS, stride=16), :] = block
    send_ref[...] = t_scr[...].reshape(CHIPS, 16, 128).astype(BF16)


def row_call(core_ref, here_ref, q, own, pair, wk, wv, wide, g, mine, wo):
    half, keys = mine.shape[1], own.shape[0]
    return call(
        row_kernel,
        jax.ShapeDtypeStruct((CHIPS, 16, 128), BF16),
        core_ref,
        here_ref,
        q,
        own,
        pair,
        wk,
        wv,
        wide,
        g,
        mine,
        wo,
        smem=2,
        scratch=[
            pltpu.VMEM((2, HEADS * half, keys), F32),
            pltpu.VMEM((2, HEADS * half, keys), BF16),
            pltpu.VMEM((2, keys, FEATURES), BF16),
            pltpu.VMEM((CHIPS * 16, 128), F32),
        ],
        flops=2 * 2 * 2 * HEADS * half * keys * FEATURES,
        size=6 * 2**20,
        vmem=20,
    )


def column_kernel(x_ref, wq_ref, wk_ref, wv_ref, wg_ref, wo_ref, out_ref, t_scr, u_scr):
    t_scr[...] = x_ref[...].astype(F32).reshape(CHIPS * 16, 128)
    part = [t_scr[pl.ds(i, CHIPS, stride=16), :] for i in range(16)]
    count = 2 * CHIPS

    def tokens_of(kind):
        rows = [
            jnp.concatenate([part[kind * 8 + s * 4 + rr * 2], part[kind * 8 + s * 4 + rr * 2 + 1]], axis=1)
            for rr in range(2)
            for s in range(2)
        ]
        return jnp.concatenate(rows, axis=0)

    tokens = tokens_of(0).astype(BF16)
    q = matmul(tokens, wq_ref[...])
    k = matmul(tokens, wk_ref[...]).astype(BF16)
    v = matmul(tokens, wv_ref[...]).astype(BF16)
    g = jax.nn.sigmoid(matmul(tokens, wg_ref[...]))
    gated = []
    for rr in range(2):
        lo, hi = rr * count, (rr + 1) * count
        masked = jnp.concatenate(
            [jnp.where(head_mask((count, FEATURES), h), q[lo:hi], 0.0) for h in range(HEADS)], axis=0
        ).astype(BF16)
        logits = lax.dot_general(masked, k[lo:hi], NT, preferred_element_type=F32) * SCALE
        e = jnp.exp(logits - jnp.max(logits, axis=-1, keepdims=True))
        share = 1.0 / jnp.sum(e, axis=-1, keepdims=True)
        out = matmul(e.astype(BF16), v[lo:hi]) * share
        attended = jnp.zeros((count, FEATURES), F32)
        for h in range(HEADS):
            attended = jnp.where(
                head_mask(attended.shape, h), out[h * count : (h + 1) * count], attended
            )
        gated.append((g[lo:hi] * attended).astype(BF16))
    update = tokens_of(1) + matmul(jnp.concatenate(gated, axis=0), wo_ref[...])
    for rr in range(2):
        for s in range(2):
            at = (rr * 2 + s) * CHIPS
            for half in range(2):
                u_scr[pl.ds(s * CHIPS * 4 + rr * 2 + half, CHIPS, stride=4), :] = update[
                    at : at + CHIPS, half * 128 : (half + 1) * 128
                ]
    out_ref[...] = u_scr[...].astype(BF16)


def final_kernel(x_ref, rows_ref, out_ref, t_scr):
    t_scr[...] = x_ref[...].astype(F32)
    part = [t_scr[pl.ds(s * CHIPS * 4 + i, CHIPS, stride=4), :] for s in range(2) for i in range(4)]
    step = rows_ref.shape[0] // (2 * ZH)
    for s in range(2):
        update = jnp.concatenate(
            [jnp.concatenate([part[s * 4 + rr * 2], part[s * 4 + rr * 2 + 1]], axis=1) for rr in range(2)],
            axis=0,
        )
        for z in range(ZH):
            at = (z * 2 + s) * step
            out_ref[at : at + step] = rows_ref[at : at + step] + update[z * step : (z + 1) * step]


def shards(
    alignment,
    pair,
    offset_matrix,
    row_wq,
    row_wk,
    row_wv,
    row_wg,
    row_wo,
    col_wq,
    col_wk,
    col_wv,
    col_wg,
    col_wo,
):
    core = lax.axis_index("c").astype(jnp.int32)
    core_ref = core.reshape(1)
    tokens = alignment.shape[1]
    half = tokens // 2
    swap = [(0, 1), (1, 0)]
    turn = [
        (b * BLOCKS + r, (b ^ TURN[b ^ r]) * BLOCKS + b) for b in range(BLOCKS) for r in range(BLOCKS)
    ]

    pair_shape = pair.shape
    bias_shape = (HEADS, pair_shape[0], pair_shape[1])
    bias_here = call(
        pair_kernel,
        jax.ShapeDtypeStruct(bias_shape, BF16),
        offset_matrix.T,
        pair,
        hbm=2,
        scratch=[
            pltpu.VMEM((HEADS, pair_shape[2]), F32),
            pltpu.VMEM(pair_shape, F32),
            pltpu.VMEM(bias_shape, F32),
            pltpu.SemaphoreType.DMA((2,)),
        ],
    )
    bias = lax.ppermute(bias_here, ("y", "zl", "x"), turn)
    normed = call(norm_kernel, jax.ShapeDtypeStruct((tokens, FEATURES), BF16), alignment[0])
    near_normed = lax.all_gather(normed, "zl", axis=0, tiled=True)
    near_normed, bias = lax.optimization_barrier((near_normed, bias))
    own_normed = lax.all_gather(near_normed, "x", axis=0, tiled=True)
    pair_normed = lax.ppermute(own_normed, "c", swap)
    rows = lax.all_gather(alignment, "c", axis=0, tiled=True)
    rows = rows.reshape(2, ZH, 2, half // ZH, FEATURES)

    wide = jnp.broadcast_to(bias[None], (CHIPS,) + bias.shape)
    wide = lax.all_to_all(wide, ("y", "zh"), 0, 0, tiled=True)

    here_ref = lax.axis_index(RES).astype(jnp.int32).reshape(1)
    q, g, mine = call(
        query_kernel,
        (
            jax.ShapeDtypeStruct((2, half, FEATURES), BF16),
            jax.ShapeDtypeStruct((2, half, FEATURES), F32),
            jax.ShapeDtypeStruct((2, half, FEATURES), F32),
        ),
        core_ref,
        rows,
        row_wq,
        row_wg,
        smem=1,
        flops=2 * 2 * half * FEATURES * 2 * FEATURES,
        size=2**20,
    )
    send = row_call(
        core_ref, here_ref, q, own_normed, pair_normed, row_wk, row_wv, wide, g, mine, row_wo
    )

    block = lax.all_to_all(send, ("zh", "y"), 0, 0, tiled=True)
    update = call(
        column_kernel,
        jax.ShapeDtypeStruct((CHIPS * 8, 128), BF16),
        block,
        col_wq,
        col_wk,
        col_wv,
        col_wg,
        col_wo,
        scratch=[pltpu.VMEM((CHIPS * 16, 128), F32), pltpu.VMEM((CHIPS * 8, 128), F32)],
    )
    back = lax.all_to_all(update.reshape(2 * CHIPS, 4, 128), ("c", "zh", "y"), 0, 0, tiled=True)
    out = call(
        final_kernel,
        jax.ShapeDtypeStruct((tokens, FEATURES), F32),
        back.reshape(CHIPS * 8, 128),
        alignment[0],
        scratch=[pltpu.VMEM((CHIPS * 8, 128), F32)],
    )
    return out[None]


def solution(mesh):
    fine = Mesh(mesh.devices.reshape(Y, ZH, C, ZL, X), ("y", "zh", "c", "zl", "x"))
    split = P(SEQ, RES, None)
    in_specs = (split, split) + (P(),) * 11
    return jax.shard_map(shards, mesh=fine, in_specs=in_specs, out_specs=split, check_vma=False)
```

```python
import functools

import jax
import jax.numpy as jnp
from jax import lax
from jax.experimental import pallas as pl
from jax.experimental.pallas import tpu as pltpu
from jax.sharding import Mesh, PartitionSpec as P

EPS = 1e-05
HEADS = 8
HEAD_SIZE = 32
FEATURES = HEADS * HEAD_SIZE
SCALE = HEAD_SIZE ** (-0.5)
Y, ZH, C, ZL, X = 8, 4, 2, 2, 4
SEQ = ("y", "zh", "c")
RES = ("zl", "x")
CHIPS = Y * ZH
BLOCKS = ZL * X
TURN = (4, 3, 1, 5, 7, 2, 0, 6)
TURN_BITS = sum(y << (4 * n) for n, y in enumerate(TURN))
VMEM = pl.BlockSpec(memory_space=pltpu.VMEM)
SMEM = pl.BlockSpec(memory_space=pltpu.SMEM)
HBM = pl.BlockSpec(memory_space=pltpu.HBM)
NT = (((1,), (1,)), ((), ()))
F32, BF16 = jnp.float32, jnp.bfloat16


def call(kernel, out_shape, *args, scratch=(), smem=0, hbm=0, flops=0, size=0, vmem=6):
    vmem_count = len(args) - smem - hbm
    pinned = [pltpu.with_memory_space_constraint(x, pltpu.HBM) for x in args[len(args) - hbm :]]
    return pl.pallas_call(
        kernel,
        out_shape=out_shape,
        in_specs=[SMEM] * smem + [VMEM] * vmem_count + [HBM] * hbm,
        out_specs=jax.tree.map(lambda _: VMEM, out_shape),
        scratch_shapes=list(scratch),
        compiler_params=pltpu.CompilerParams(vmem_limit_bytes=vmem * 2**20),
        cost_estimate=pl.CostEstimate(flops=flops, bytes_accessed=size, transcendentals=0),
    )(*args[: len(args) - hbm], *pinned)


def standardize(rows):
    centre = jnp.mean(rows, axis=-1, keepdims=True)
    moved = rows - centre
    spread = jnp.mean(moved * moved, axis=-1, keepdims=True)
    return moved * lax.rsqrt(spread + EPS)


def matmul(a, b):
    return jnp.dot(a, b, preferred_element_type=F32)


def head_mask(shape, head):
    lane = lax.broadcasted_iota(jnp.int32, shape, 1)
    return (lane >= head * HEAD_SIZE) & (lane < (head + 1) * HEAD_SIZE)


def pair_kernel(w_hbm, x_ref, out_ref, w_ref, x_scr, scr, sems):
    count = x_ref.shape[0]
    parts = sems.shape[0] - 1
    step = count // parts
    first = pltpu.make_async_copy(w_hbm, w_ref, sems.at[parts])
    first.start()
    copies = []
    for n in range(parts):
        part = pl.ds(n * step, step)
        copies.append(pltpu.make_async_copy(x_ref.at[part], x_scr.at[part], sems.at[n]))
        copies[n].start()
    first.wait()
    w = w_ref[...]
    wh = w.astype(BF16)
    wl = (w - wh.astype(F32)).astype(BF16)
    top = jnp.concatenate([wh.astype(F32), wh.astype(F32)], axis=1)
    low = jnp.concatenate([wl.astype(F32), jnp.zeros_like(w)], axis=1)
    weights = jnp.concatenate([top, low], axis=0).astype(BF16)
    for i in range(count):
        if i % step == 0:
            copies[i // step].wait()
        d = standardize(x_scr[i])
        dh = d.astype(BF16)
        dl = (d - dh.astype(F32)).astype(BF16)
        both = jnp.concatenate([dh, dl], axis=1)
        part = lax.dot_general(weights, both, NT, preferred_element_type=F32)
        scr[:, i, :] = part[:HEADS] + part[HEADS:]
    out_ref[...] = scr[...].astype(BF16)


def norm_kernel(x_ref, out_ref):
    out_ref[...] = standardize(x_ref[...]).astype(BF16)


def query_kernel(c_ref, rows_ref, wq_ref, wg_ref, q_ref, g_ref, mine_ref):
    core = c_ref[0]
    mine = jnp.concatenate([rows_ref[core, :, core], rows_ref[1 - core, :, core]], axis=0)
    mine = mine.reshape(-1, FEATURES)
    mine_ref[...] = mine.reshape(mine_ref.shape)
    tokens = standardize(mine).astype(BF16)
    g_ref[...] = jax.nn.sigmoid(matmul(tokens, wg_ref[...])).reshape(g_ref.shape)
    q_ref[...] = matmul(tokens, wq_ref[...]).astype(BF16).reshape(q_ref.shape)


def row_kernel(
    c_ref, here_ref, q_ref, own_ref, pair_ref, wk_ref, wv_ref, bias_ref, g_ref, rows_ref, wo_ref,
    send_ref, s_scr, p_scr, v_scr, t_scr
):
    count = rows_ref.shape[1]
    keys = own_ref.shape[0]
    cols = keys // BLOCKS
    here = here_ref[0]
    at = []
    for n in range(BLOCKS):
        block = (n % ZL) * X + n // ZL
        at.append((here ^ ((TURN_BITS >> (4 * (here ^ block))) & 7)) * ZH)
    gated, outs, shares = [], [], []

    def softmax(s):
        for h in range(HEADS):
            lo, hi = h * count, (h + 1) * count
            logits = []
            for n in range(BLOCKS):
                bias = bias_ref[pl.ds(at[n], ZH), h].astype(F32).reshape(count, cols)
                logits.append(s_scr[s, lo:hi, n * cols : (n + 1) * cols] * SCALE + bias)
            top = functools.reduce(jnp.maximum, logits)
            top = jnp.max(top, axis=-1, keepdims=True)
            total = None
            for n in range(BLOCKS):
                e = jnp.exp(logits[n] - top)
                total = e if total is None else total + e
                p_scr[s, lo:hi, n * cols : (n + 1) * cols] = e.astype(BF16)
            shares.append(1.0 / jnp.sum(total, axis=-1, keepdims=True))

    for s, ref in enumerate((own_ref, pair_ref)):
        tokens = ref[...]
        k = matmul(tokens, wk_ref[...]).astype(BF16)
        v_scr[s] = matmul(tokens, wv_ref[...]).astype(BF16)
        q = q_ref[s].astype(F32)
        masked = [jnp.where(head_mask(q.shape, h), q, 0.0).astype(BF16) for h in range(HEADS)]
        masked = jnp.concatenate(masked, axis=0)
        s_scr[s] = lax.dot_general(masked, k, NT, preferred_element_type=F32)
    for s in range(2):
        softmax(s)
        outs.append(matmul(p_scr[s], v_scr[s]))
    for s in range(2):
        attended = jnp.zeros((count, FEATURES), F32)
        for h in range(HEADS):
            part = outs[s][h * count : (h + 1) * count] * shares[s * HEADS + h]
            attended = jnp.where(head_mask(attended.shape, h), part, attended)
        gated.append((g_ref[s] * attended).astype(BF16))
    delta = matmul(jnp.concatenate(gated, axis=0), wo_ref[...])
    first = c_ref[0] == 0
    own, pair = [rows_ref[s] + delta[s * count : (s + 1) * count] for s in range(2)]
    ordered = [jnp.where(first, own, pair), jnp.where(first, pair, own)]
    for s in range(2):
        for rr in range(2):
            for half in range(2):
                block = ordered[s][rr * CHIPS : (rr + 1) * CHIPS, half * 128 : (half + 1) * 128]
                t_scr[pl.ds(s * 4 + rr * 2 + half, CHIPS, stride=8), :] = block
    send_ref[...] = t_scr[...].reshape(CHIPS, 8, 128).astype(BF16)


def row_call(core_ref, here_ref, q, own, pair, wk, wv, wide, g, mine, wo):
    half, keys = mine.shape[1], own.shape[0]
    return call(
        row_kernel,
        jax.ShapeDtypeStruct((CHIPS, 8, 128), BF16),
        core_ref,
        here_ref,
        q,
        own,
        pair,
        wk,
        wv,
        wide,
        g,
        mine,
        wo,
        smem=2,
        scratch=[
            pltpu.VMEM((2, HEADS * half, keys), F32),
            pltpu.VMEM((2, HEADS * half, keys), BF16),
            pltpu.VMEM((2, keys, FEATURES), BF16),
            pltpu.VMEM((CHIPS * 8, 128), F32),
        ],
        flops=2 * 2 * 2 * HEADS * half * keys * FEATURES,
        size=6 * 2**20,
        vmem=20,
    )


def column_kernel(x_ref, wq_ref, wk_ref, wv_ref, wg_ref, wo_ref, out_ref, t_scr):
    t_scr[...] = x_ref[...].astype(F32).reshape(CHIPS * 8, 128)
    part = [t_scr[pl.ds(i, CHIPS, stride=8), :] for i in range(8)]
    count = 2 * CHIPS
    rows = [
        jnp.concatenate([part[s * 4 + rr * 2], part[s * 4 + rr * 2 + 1]], axis=1)
        for rr in range(2)
        for s in range(2)
    ]
    middle = jnp.concatenate(rows, axis=0)
    tokens = standardize(middle).astype(BF16)
    q = matmul(tokens, wq_ref[...])
    k = matmul(tokens, wk_ref[...]).astype(BF16)
    v = matmul(tokens, wv_ref[...]).astype(BF16)
    g = jax.nn.sigmoid(matmul(tokens, wg_ref[...]))
    gated = []
    for rr in range(2):
        lo, hi = rr * count, (rr + 1) * count
        masked = jnp.concatenate(
            [jnp.where(head_mask((count, FEATURES), h), q[lo:hi], 0.0) for h in range(HEADS)], axis=0
        ).astype(BF16)
        logits = lax.dot_general(masked, k[lo:hi], NT, preferred_element_type=F32) * SCALE
        e = jnp.exp(logits - jnp.max(logits, axis=-1, keepdims=True))
        share = 1.0 / jnp.sum(e, axis=-1, keepdims=True)
        out = matmul(e.astype(BF16), v[lo:hi]) * share
        attended = jnp.zeros((count, FEATURES), F32)
        for h in range(HEADS):
            attended = jnp.where(
                head_mask(attended.shape, h), out[h * count : (h + 1) * count], attended
            )
        gated.append((g[lo:hi] * attended).astype(BF16))
    result = middle + matmul(jnp.concatenate(gated, axis=0), wo_ref[...])
    for rr in range(2):
        for s in range(2):
            at = (rr * 2 + s) * CHIPS
            for half in range(2):
                t_scr[pl.ds(s * CHIPS * 4 + rr * 2 + half, CHIPS, stride=4), :] = result[
                    at : at + CHIPS, half * 128 : (half + 1) * 128
                ]
    out_ref[...] = t_scr[...].astype(BF16)


def final_kernel(x_ref, out_ref, t_scr):
    t_scr[...] = x_ref[...].astype(F32)
    part = [t_scr[pl.ds(s * CHIPS * 4 + i, CHIPS, stride=4), :] for s in range(2) for i in range(4)]
    step = out_ref.shape[0] // (2 * ZH)
    for s in range(2):
        rows = jnp.concatenate(
            [jnp.concatenate([part[s * 4 + rr * 2], part[s * 4 + rr * 2 + 1]], axis=1) for rr in range(2)],
            axis=0,
        )
        for z in range(ZH):
            at = (z * 2 + s) * step
            out_ref[at : at + step] = rows[z * step : (z + 1) * step]


def shards(
    alignment,
    pair,
    offset_matrix,
    row_wq,
    row_wk,
    row_wv,
    row_wg,
    row_wo,
    col_wq,
    col_wk,
    col_wv,
    col_wg,
    col_wo,
):
    core = lax.axis_index("c").astype(jnp.int32)
    core_ref = core.reshape(1)
    tokens = alignment.shape[1]
    half = tokens // 2
    swap = [(0, 1), (1, 0)]
    turn = [
        (b * BLOCKS + r, (b ^ TURN[b ^ r]) * BLOCKS + b) for b in range(BLOCKS) for r in range(BLOCKS)
    ]

    pair_shape = pair.shape
    bias_shape = (HEADS, pair_shape[0], pair_shape[1])
    bias_here = call(
        pair_kernel,
        jax.ShapeDtypeStruct(bias_shape, BF16),
        offset_matrix.T,
        pair,
        hbm=2,
        scratch=[
            pltpu.VMEM((HEADS, pair_shape[2]), F32),
            pltpu.VMEM(pair_shape, F32),
            pltpu.VMEM(bias_shape, F32),
            pltpu.SemaphoreType.DMA((2,)),
        ],
    )
    bias = lax.ppermute(bias_here, ("y", "zl", "x"), turn)
    normed = call(norm_kernel, jax.ShapeDtypeStruct((tokens, FEATURES), BF16), alignment[0])
    near_normed = lax.all_gather(normed, "zl", axis=0, tiled=True)
    near_normed, bias = lax.optimization_barrier((near_normed, bias))
    own_normed = lax.all_gather(near_normed, "x", axis=0, tiled=True)
    pair_normed = lax.ppermute(own_normed, "c", swap)
    rows = lax.all_gather(alignment, "c", axis=0, tiled=True)
    rows = rows.reshape(2, ZH, 2, half // ZH, FEATURES)

    wide = jnp.broadcast_to(bias[None], (CHIPS,) + bias.shape)
    wide = lax.all_to_all(wide, ("y", "zh"), 0, 0, tiled=True)

    here_ref = lax.axis_index(RES).astype(jnp.int32).reshape(1)
    q, g, mine = call(
        query_kernel,
        (
            jax.ShapeDtypeStruct((2, half, FEATURES), BF16),
            jax.ShapeDtypeStruct((2, half, FEATURES), F32),
            jax.ShapeDtypeStruct((2, half, FEATURES), F32),
        ),
        core_ref,
        rows,
        row_wq,
        row_wg,
        smem=1,
        flops=2 * 2 * half * FEATURES * 2 * FEATURES,
        size=2**20,
    )
    send = row_call(
        core_ref, here_ref, q, own_normed, pair_normed, row_wk, row_wv, wide, g, mine, row_wo
    )

    block = lax.all_to_all(send, ("zh", "y"), 0, 0, tiled=True)
    result = call(
        column_kernel,
        jax.ShapeDtypeStruct((CHIPS * 8, 128), BF16),
        block,
        col_wq,
        col_wk,
        col_wv,
        col_wg,
        col_wo,
        scratch=[pltpu.VMEM((CHIPS * 8, 128), F32)],
    )
    back = lax.all_to_all(result.reshape(2 * CHIPS, 4, 128), ("c", "zh", "y"), 0, 0, tiled=True)
    out = call(
        final_kernel,
        jax.ShapeDtypeStruct((tokens, FEATURES), F32),
        back.reshape(CHIPS * 8, 128),
        scratch=[pltpu.VMEM((CHIPS * 8, 128), F32)],
    )
    return out[None]


def solution(mesh):
    fine = Mesh(mesh.devices.reshape(Y, ZH, C, ZL, X), ("y", "zh", "c", "zl", "x"))
    split = P(SEQ, RES, None)
    in_specs = (split, split) + (P(),) * 11
    return jax.shard_map(shards, mesh=fine, in_specs=in_specs, out_specs=split, check_vma=False)
```

```python
import functools

import jax
import jax.numpy as jnp
from jax import lax
from jax.experimental import pallas as pl
from jax.experimental.pallas import tpu as pltpu
from jax.sharding import Mesh, PartitionSpec as P

EPS = 1e-05
HEADS = 8
HEAD_SIZE = 32
FEATURES = HEADS * HEAD_SIZE
SCALE = HEAD_SIZE ** (-0.5)
Y, ZH, C, ZL, X = 8, 4, 2, 2, 4
SEQ = ("y", "zh", "c")
RES = ("zl", "x")
CHIPS = Y * ZH
BLOCKS = ZL * X
TURN = (4, 3, 1, 5, 7, 2, 0, 6)
TURN_BITS = sum(y << (4 * n) for n, y in enumerate(TURN))
VMEM = pl.BlockSpec(memory_space=pltpu.VMEM)
SMEM = pl.BlockSpec(memory_space=pltpu.SMEM)
HBM = pl.BlockSpec(memory_space=pltpu.HBM)
NT = (((1,), (1,)), ((), ()))
F32, BF16 = jnp.float32, jnp.bfloat16


def call(kernel, out_shape, *args, scratch=(), smem=0, hbm=0, flops=0, size=0, vmem=6):
    vmem_count = len(args) - smem - hbm
    pinned = [pltpu.with_memory_space_constraint(x, pltpu.HBM) for x in args[len(args) - hbm :]]
    return pl.pallas_call(
        kernel,
        out_shape=out_shape,
        in_specs=[SMEM] * smem + [VMEM] * vmem_count + [HBM] * hbm,
        out_specs=jax.tree.map(lambda _: VMEM, out_shape),
        scratch_shapes=list(scratch),
        compiler_params=pltpu.CompilerParams(vmem_limit_bytes=vmem * 2**20),
        cost_estimate=pl.CostEstimate(flops=flops, bytes_accessed=size, transcendentals=0),
    )(*args[: len(args) - hbm], *pinned)


def standardize(rows):
    centre = jnp.mean(rows, axis=-1, keepdims=True)
    moved = rows - centre
    spread = jnp.mean(moved * moved, axis=-1, keepdims=True)
    return moved * lax.rsqrt(spread + EPS)


def matmul(a, b):
    return jnp.dot(a, b, preferred_element_type=F32)


def head_mask(shape, head):
    lane = lax.broadcasted_iota(jnp.int32, shape, 1)
    return (lane >= head * HEAD_SIZE) & (lane < (head + 1) * HEAD_SIZE)


def pair_kernel(w_hbm, x_ref, out_ref, w_ref, x_scr, scr, sems):
    count = x_ref.shape[0]
    parts = sems.shape[0] - 1
    step = count // parts
    copies = []
    for n in range(parts):
        part = pl.ds(n * step, step)
        copies.append(pltpu.make_async_copy(x_ref.at[part], x_scr.at[part], sems.at[n]))
        copies[n].start()
    first = pltpu.make_async_copy(w_hbm, w_ref, sems.at[parts])
    first.start()
    first.wait()
    w = w_ref[...]
    wh = w.astype(BF16)
    wl = (w - wh.astype(F32)).astype(BF16)
    top = jnp.concatenate([wh.astype(F32), wh.astype(F32)], axis=1)
    low = jnp.concatenate([wl.astype(F32), jnp.zeros_like(w)], axis=1)
    weights = jnp.concatenate([top, low], axis=0).astype(BF16)
    for copy in copies:
        copy.wait()
    for i in range(count):
        d = standardize(x_scr[i])
        dh = d.astype(BF16)
        dl = (d - dh.astype(F32)).astype(BF16)
        both = jnp.concatenate([dh, dl], axis=1)
        part = lax.dot_general(weights, both, NT, preferred_element_type=F32)
        scr[:, i, :] = part[:HEADS] + part[HEADS:]
    out_ref[...] = scr[...].astype(BF16)


def norm_kernel(x_ref, out_ref):
    out_ref[...] = standardize(x_ref[...]).astype(BF16)


def query_kernel(c_ref, rows_ref, wq_ref, wg_ref, q_ref, g_ref, mine_ref):
    core = c_ref[0]
    mine = jnp.concatenate([rows_ref[core, :, core], rows_ref[1 - core, :, core]], axis=0)
    mine = mine.reshape(-1, FEATURES)
    mine_ref[...] = mine.reshape(mine_ref.shape)
    tokens = standardize(mine).astype(BF16)
    g_ref[...] = jax.nn.sigmoid(matmul(tokens, wg_ref[...])).reshape(g_ref.shape)
    q_ref[...] = matmul(tokens, wq_ref[...]).astype(BF16).reshape(q_ref.shape)


def row_kernel(
    c_ref, here_ref, q_ref, own_ref, pair_ref, wk_ref, wv_ref, bias_ref, g_ref, rows_ref, wo_ref,
    send_ref, s_scr, p_scr, v_scr, t_scr
):
    count = rows_ref.shape[1]
    keys = own_ref.shape[0]
    cols = keys // BLOCKS
    here = here_ref[0]
    at = []
    for n in range(BLOCKS):
        block = (n % ZL) * X + n // ZL
        at.append((here ^ ((TURN_BITS >> (4 * (here ^ block))) & 7)) * ZH)
    gated, outs, shares = [], [], []

    def softmax(s):
        for h in range(HEADS):
            lo, hi = h * count, (h + 1) * count
            logits = []
            for n in range(BLOCKS):
                bias = bias_ref[pl.ds(at[n], ZH), h].astype(F32).reshape(count, cols)
                logits.append(s_scr[s, lo:hi, n * cols : (n + 1) * cols] * SCALE + bias)
            top = functools.reduce(jnp.maximum, logits)
            top = jnp.max(top, axis=-1, keepdims=True)
            total = None
            for n in range(BLOCKS):
                e = jnp.exp(logits[n] - top)
                total = e if total is None else total + e
                p_scr[s, lo:hi, n * cols : (n + 1) * cols] = e.astype(BF16)
            shares.append(1.0 / jnp.sum(total, axis=-1, keepdims=True))

    def prepare(s, ref):
        tokens = ref[...]
        k = matmul(tokens, wk_ref[...]).astype(BF16)
        v_scr[s] = matmul(tokens, wv_ref[...]).astype(BF16)
        q = q_ref[s].astype(F32)
        masked = [jnp.where(head_mask(q.shape, h), q, 0.0).astype(BF16) for h in range(HEADS)]
        masked = jnp.concatenate(masked, axis=0)
        s_scr[s] = lax.dot_general(masked, k, NT, preferred_element_type=F32)

    prepare(0, own_ref)
    softmax(0)
    prepare(1, pair_ref)
    outs.append(matmul(p_scr[0], v_scr[0]))
    softmax(1)
    outs.append(matmul(p_scr[1], v_scr[1]))
    for s in range(2):
        attended = jnp.zeros((count, FEATURES), F32)
        for h in range(HEADS):
            part = outs[s][h * count : (h + 1) * count] * shares[s * HEADS + h]
            attended = jnp.where(head_mask(attended.shape, h), part, attended)
        gated.append((g_ref[s] * attended).astype(BF16))
    delta = matmul(jnp.concatenate(gated, axis=0), wo_ref[...])
    first = c_ref[0] == 0
    deltas = [delta[s * count : (s + 1) * count] for s in range(2)]
    normed = [standardize(rows_ref[s] + deltas[s]) for s in range(2)]
    for kind, (own, pair) in enumerate((normed, deltas)):
        ordered = [jnp.where(first, own, pair), jnp.where(first, pair, own)]
        for s in range(2):
            for rr in range(2):
                for half in range(2):
                    block = ordered[s][rr * CHIPS : (rr + 1) * CHIPS, half * 128 : (half + 1) * 128]
                    t_scr[pl.ds(kind * 8 + s * 4 + rr * 2 + half, CHIPS, stride=16), :] = block
    send_ref[...] = t_scr[...].reshape(CHIPS, 16, 128).astype(BF16)


def row_call(core_ref, here_ref, q, own, pair, wk, wv, wide, g, mine, wo):
    half, keys = mine.shape[1], own.shape[0]
    return call(
        row_kernel,
        jax.ShapeDtypeStruct((CHIPS, 16, 128), BF16),
        core_ref,
        here_ref,
        q,
        own,
        pair,
        wk,
        wv,
        wide,
        g,
        mine,
        wo,
        smem=2,
        scratch=[
            pltpu.VMEM((2, HEADS * half, keys), F32),
            pltpu.VMEM((2, HEADS * half, keys), BF16),
            pltpu.VMEM((2, keys, FEATURES), BF16),
            pltpu.VMEM((CHIPS * 16, 128), F32),
        ],
        flops=2 * 2 * 2 * HEADS * half * keys * FEATURES,
        size=6 * 2**20,
        vmem=20,
    )


def column_kernel(x_ref, wq_ref, wk_ref, wv_ref, wg_ref, wo_ref, out_ref, t_scr, u_scr):
    t_scr[...] = x_ref[...].astype(F32).reshape(CHIPS * 16, 128)
    part = [t_scr[pl.ds(i, CHIPS, stride=16), :] for i in range(16)]
    count = 2 * CHIPS

    def tokens_of(kind):
        rows = [
            jnp.concatenate([part[kind * 8 + s * 4 + rr * 2], part[kind * 8 + s * 4 + rr * 2 + 1]], axis=1)
            for rr in range(2)
            for s in range(2)
        ]
        return jnp.concatenate(rows, axis=0)

    tokens = tokens_of(0).astype(BF16)
    q = matmul(tokens, wq_ref[...])
    k = matmul(tokens, wk_ref[...]).astype(BF16)
    v = matmul(tokens, wv_ref[...]).astype(BF16)
    g = jax.nn.sigmoid(matmul(tokens, wg_ref[...]))
    gated = []
    for rr in range(2):
        lo, hi = rr * count, (rr + 1) * count
        masked = jnp.concatenate(
            [jnp.where(head_mask((count, FEATURES), h), q[lo:hi], 0.0) for h in range(HEADS)], axis=0
        ).astype(BF16)
        logits = lax.dot_general(masked, k[lo:hi], NT, preferred_element_type=F32) * SCALE
        e = jnp.exp(logits - jnp.max(logits, axis=-1, keepdims=True))
        share = 1.0 / jnp.sum(e, axis=-1, keepdims=True)
        out = matmul(e.astype(BF16), v[lo:hi]) * share
        attended = jnp.zeros((count, FEATURES), F32)
        for h in range(HEADS):
            attended = jnp.where(
                head_mask(attended.shape, h), out[h * count : (h + 1) * count], attended
            )
        gated.append((g[lo:hi] * attended).astype(BF16))
    update = tokens_of(1) + matmul(jnp.concatenate(gated, axis=0), wo_ref[...])
    for rr in range(2):
        for s in range(2):
            at = (rr * 2 + s) * CHIPS
            for half in range(2):
                u_scr[pl.ds(s * CHIPS * 4 + rr * 2 + half, CHIPS, stride=4), :] = update[
                    at : at + CHIPS, half * 128 : (half + 1) * 128
                ]
    out_ref[...] = u_scr[...].astype(BF16)


def final_kernel(x_ref, rows_ref, out_ref, t_scr):
    t_scr[...] = x_ref[...].astype(F32)
    part = [t_scr[pl.ds(s * CHIPS * 4 + i, CHIPS, stride=4), :] for s in range(2) for i in range(4)]
    step = rows_ref.shape[0] // (2 * ZH)
    for s in range(2):
        update = jnp.concatenate(
            [jnp.concatenate([part[s * 4 + rr * 2], part[s * 4 + rr * 2 + 1]], axis=1) for rr in range(2)],
            axis=0,
        )
        for z in range(ZH):
            at = (z * 2 + s) * step
            out_ref[at : at + step] = rows_ref[at : at + step] + update[z * step : (z + 1) * step]


def shards(
    alignment,
    pair,
    offset_matrix,
    row_wq,
    row_wk,
    row_wv,
    row_wg,
    row_wo,
    col_wq,
    col_wk,
    col_wv,
    col_wg,
    col_wo,
):
    core = lax.axis_index("c").astype(jnp.int32)
    core_ref = core.reshape(1)
    tokens = alignment.shape[1]
    half = tokens // 2
    swap = [(0, 1), (1, 0)]
    turn = [
        (b * BLOCKS + r, (b ^ TURN[b ^ r]) * BLOCKS + b) for b in range(BLOCKS) for r in range(BLOCKS)
    ]

    pair_shape = pair.shape
    bias_shape = (HEADS, pair_shape[0], pair_shape[1])
    bias_here = call(
        pair_kernel,
        jax.ShapeDtypeStruct(bias_shape, BF16),
        offset_matrix.T,
        pair,
        hbm=2,
        scratch=[
            pltpu.VMEM((HEADS, pair_shape[2]), F32),
            pltpu.VMEM(pair_shape, F32),
            pltpu.VMEM(bias_shape, F32),
            pltpu.SemaphoreType.DMA((3,)),
        ],
    )
    bias = lax.ppermute(bias_here, ("y", "zl", "x"), turn)
    normed = call(norm_kernel, jax.ShapeDtypeStruct((tokens, FEATURES), BF16), alignment[0])
    near_normed = lax.all_gather(normed, "zl", axis=0, tiled=True)
    near_normed, bias = lax.optimization_barrier((near_normed, bias))
    own_normed = lax.all_gather(near_normed, "x", axis=0, tiled=True)
    pair_normed = lax.ppermute(own_normed, "c", swap)
    rows = lax.all_gather(alignment, "c", axis=0, tiled=True)
    rows = rows.reshape(2, ZH, 2, half // ZH, FEATURES)

    wide = jnp.broadcast_to(bias[None], (CHIPS,) + bias.shape)
    wide = lax.all_to_all(wide, ("y", "zh"), 0, 0, tiled=True)

    here_ref = lax.axis_index(RES).astype(jnp.int32).reshape(1)
    q, g, mine = call(
        query_kernel,
        (
            jax.ShapeDtypeStruct((2, half, FEATURES), BF16),
            jax.ShapeDtypeStruct((2, half, FEATURES), F32),
            jax.ShapeDtypeStruct((2, half, FEATURES), F32),
        ),
        core_ref,
        rows,
        row_wq,
        row_wg,
        smem=1,
        flops=2 * 2 * half * FEATURES * 2 * FEATURES,
        size=2**20,
    )
    send = row_call(
        core_ref, here_ref, q, own_normed, pair_normed, row_wk, row_wv, wide, g, mine, row_wo
    )

    block = lax.all_to_all(send, ("zh", "y"), 0, 0, tiled=True)
    update = call(
        column_kernel,
        jax.ShapeDtypeStruct((CHIPS * 8, 128), BF16),
        block,
        col_wq,
        col_wk,
        col_wv,
        col_wg,
        col_wo,
        scratch=[pltpu.VMEM((CHIPS * 16, 128), F32), pltpu.VMEM((CHIPS * 8, 128), F32)],
    )
    back = lax.all_to_all(update.reshape(2 * CHIPS, 4, 128), ("c", "zh", "y"), 0, 0, tiled=True)
    out = call(
        final_kernel,
        jax.ShapeDtypeStruct((tokens, FEATURES), F32),
        back.reshape(CHIPS * 8, 128),
        alignment[0],
        scratch=[pltpu.VMEM((CHIPS * 8, 128), F32)],
    )
    return out[None]


def solution(mesh):
    fine = Mesh(mesh.devices.reshape(Y, ZH, C, ZL, X), ("y", "zh", "c", "zl", "x"))
    split = P(SEQ, RES, None)
    in_specs = (split, split) + (P(),) * 11
    return jax.shard_map(shards, mesh=fine, in_specs=in_specs, out_specs=split, check_vma=False)
```

```python
import functools

import jax
import jax.numpy as jnp
from jax import lax
from jax.experimental import pallas as pl
from jax.experimental.pallas import tpu as pltpu
from jax.sharding import Mesh, PartitionSpec as P

EPS = 1e-05
HEADS = 8
HEAD_SIZE = 32
FEATURES = HEADS * HEAD_SIZE
SCALE = HEAD_SIZE ** (-0.5)
Y, ZH, C, ZL, X = 8, 4, 2, 2, 4
SEQ = ("y", "zh", "c")
RES = ("zl", "x")
CHIPS = Y * ZH
BLOCKS = ZL * X
TURN = (4, 2, 1, 3, 6, 5, 0, 7)
TURN_BITS = sum(y << (4 * n) for n, y in enumerate(TURN))
VMEM = pl.BlockSpec(memory_space=pltpu.VMEM)
SMEM = pl.BlockSpec(memory_space=pltpu.SMEM)
HBM = pl.BlockSpec(memory_space=pltpu.HBM)
NT = (((1,), (1,)), ((), ()))
F32, BF16 = jnp.float32, jnp.bfloat16


def call(kernel, out_shape, *args, scratch=(), smem=0, hbm=0, flops=0, size=0, vmem=6):
    vmem_count = len(args) - smem - hbm
    pinned = [pltpu.with_memory_space_constraint(x, pltpu.HBM) for x in args[len(args) - hbm :]]
    return pl.pallas_call(
        kernel,
        out_shape=out_shape,
        in_specs=[SMEM] * smem + [VMEM] * vmem_count + [HBM] * hbm,
        out_specs=jax.tree.map(lambda _: VMEM, out_shape),
        scratch_shapes=list(scratch),
        compiler_params=pltpu.CompilerParams(vmem_limit_bytes=vmem * 2**20),
        cost_estimate=pl.CostEstimate(flops=flops, bytes_accessed=size, transcendentals=0),
    )(*args[: len(args) - hbm], *pinned)


def standardize(rows):
    centre = jnp.mean(rows, axis=-1, keepdims=True)
    moved = rows - centre
    spread = jnp.mean(moved * moved, axis=-1, keepdims=True)
    return moved * lax.rsqrt(spread + EPS)


def matmul(a, b):
    return jnp.dot(a, b, preferred_element_type=F32)


def head_mask(shape, head):
    lane = lax.broadcasted_iota(jnp.int32, shape, 1)
    return (lane >= head * HEAD_SIZE) & (lane < (head + 1) * HEAD_SIZE)


def pair_kernel(w_hbm, x_ref, out_ref, w_ref, x_scr, scr, sems):
    count = x_ref.shape[0]
    parts = sems.shape[0] - 1
    step = count // parts
    copies = []
    for n in range(parts):
        part = pl.ds(n * step, step)
        copies.append(pltpu.make_async_copy(x_ref.at[part], x_scr.at[part], sems.at[n]))
        copies[n].start()
    first = pltpu.make_async_copy(w_hbm, w_ref, sems.at[parts])
    first.start()
    first.wait()
    w = w_ref[...]
    wh = w.astype(BF16)
    wl = (w - wh.astype(F32)).astype(BF16)
    top = jnp.concatenate([wh.astype(F32), wh.astype(F32)], axis=1)
    low = jnp.concatenate([wl.astype(F32), jnp.zeros_like(w)], axis=1)
    weights = jnp.concatenate([top, low], axis=0).astype(BF16)
    for copy in copies:
        copy.wait()
    for i in range(count):
        d = standardize(x_scr[i])
        dh = d.astype(BF16)
        dl = (d - dh.astype(F32)).astype(BF16)
        both = jnp.concatenate([dh, dl], axis=1)
        part = lax.dot_general(weights, both, NT, preferred_element_type=F32)
        scr[:, i, :] = part[:HEADS] + part[HEADS:]
    out_ref[...] = scr[...].astype(BF16)


def norm_kernel(x_ref, out_ref):
    out_ref[...] = standardize(x_ref[...]).astype(BF16)


def query_kernel(c_ref, rows_ref, wq_ref, wg_ref, q_ref, g_ref, mine_ref):
    core = c_ref[0]
    mine = jnp.concatenate([rows_ref[core, :, core], rows_ref[1 - core, :, core]], axis=0)
    mine = mine.reshape(-1, FEATURES)
    mine_ref[...] = mine.reshape(mine_ref.shape)
    tokens = standardize(mine).astype(BF16)
    g_ref[...] = jax.nn.sigmoid(matmul(tokens, wg_ref[...])).reshape(g_ref.shape)
    q_ref[...] = matmul(tokens, wq_ref[...]).astype(BF16).reshape(q_ref.shape)


def row_kernel(
    c_ref, here_ref, q_ref, own_ref, pair_ref, wk_ref, wv_ref, bias_ref, g_ref, rows_ref, wo_ref,
    send_ref, s_scr, p_scr, v_scr, t_scr
):
    count = rows_ref.shape[1]
    keys = own_ref.shape[0]
    cols = keys // BLOCKS
    here = here_ref[0]
    at = []
    for n in range(BLOCKS):
        block = (n % ZL) * X + n // ZL
        at.append((here ^ ((TURN_BITS >> (4 * (here ^ block))) & 7)) * ZH)
    gated, outs, shares = [], [], []

    def softmax(s):
        for h in range(HEADS):
            lo, hi = h * count, (h + 1) * count
            logits = []
            for n in range(BLOCKS):
                bias = bias_ref[pl.ds(at[n], ZH), h].astype(F32).reshape(count, cols)
                logits.append(s_scr[s, lo:hi, n * cols : (n + 1) * cols] * SCALE + bias)
            top = functools.reduce(jnp.maximum, logits)
            top = jnp.max(top, axis=-1, keepdims=True)
            total = None
            for n in range(BLOCKS):
                e = jnp.exp(logits[n] - top)
                total = e if total is None else total + e
                p_scr[s, lo:hi, n * cols : (n + 1) * cols] = e.astype(BF16)
            shares.append(1.0 / jnp.sum(total, axis=-1, keepdims=True))

    def prepare(s, ref):
        tokens = ref[...]
        k = matmul(tokens, wk_ref[...]).astype(BF16)
        v_scr[s] = matmul(tokens, wv_ref[...]).astype(BF16)
        q = q_ref[s].astype(F32)
        masked = [jnp.where(head_mask(q.shape, h), q, 0.0).astype(BF16) for h in range(HEADS)]
        masked = jnp.concatenate(masked, axis=0)
        s_scr[s] = lax.dot_general(masked, k, NT, preferred_element_type=F32)

    prepare(0, own_ref)
    softmax(0)
    prepare(1, pair_ref)
    outs.append(matmul(p_scr[0], v_scr[0]))
    softmax(1)
    outs.append(matmul(p_scr[1], v_scr[1]))
    for s in range(2):
        attended = jnp.zeros((count, FEATURES), F32)
        for h in range(HEADS):
            part = outs[s][h * count : (h + 1) * count] * shares[s * HEADS + h]
            attended = jnp.where(head_mask(attended.shape, h), part, attended)
        gated.append((g_ref[s] * attended).astype(BF16))
    delta = matmul(jnp.concatenate(gated, axis=0), wo_ref[...])
    first = c_ref[0] == 0
    deltas = [delta[s * count : (s + 1) * count] for s in range(2)]
    normed = [standardize(rows_ref[s] + deltas[s]) for s in range(2)]
    for kind, (own, pair) in enumerate((normed, deltas)):
        ordered = [jnp.where(first, own, pair), jnp.where(first, pair, own)]
        for s in range(2):
            for rr in range(2):
                for half in range(2):
                    block = ordered[s][rr * CHIPS : (rr + 1) * CHIPS, half * 128 : (half + 1) * 128]
                    t_scr[pl.ds(kind * 8 + s * 4 + rr * 2 + half, CHIPS, stride=16), :] = block
    send_ref[...] = t_scr[...].reshape(CHIPS, 16, 128).astype(BF16)


def row_call(core_ref, here_ref, q, own, pair, wk, wv, wide, g, mine, wo):
    half, keys = mine.shape[1], own.shape[0]
    return call(
        row_kernel,
        jax.ShapeDtypeStruct((CHIPS, 16, 128), BF16),
        core_ref,
        here_ref,
        q,
        own,
        pair,
        wk,
        wv,
        wide,
        g,
        mine,
        wo,
        smem=2,
        scratch=[
            pltpu.VMEM((2, HEADS * half, keys), F32),
            pltpu.VMEM((2, HEADS * half, keys), BF16),
            pltpu.VMEM((2, keys, FEATURES), BF16),
            pltpu.VMEM((CHIPS * 16, 128), F32),
        ],
        flops=2 * 2 * 2 * HEADS * half * keys * FEATURES,
        size=6 * 2**20,
        vmem=20,
    )


def column_kernel(x_ref, wq_ref, wk_ref, wv_ref, wg_ref, wo_ref, out_ref, t_scr, u_scr):
    t_scr[...] = x_ref[...].astype(F32).reshape(CHIPS * 16, 128)
    part = [t_scr[pl.ds(i, CHIPS, stride=16), :] for i in range(16)]
    count = 2 * CHIPS

    def tokens_of(kind):
        rows = [
            jnp.concatenate([part[kind * 8 + s * 4 + rr * 2], part[kind * 8 + s * 4 + rr * 2 + 1]], axis=1)
            for rr in range(2)
            for s in range(2)
        ]
        return jnp.concatenate(rows, axis=0)

    tokens = tokens_of(0).astype(BF16)
    q = matmul(tokens, wq_ref[...])
    k = matmul(tokens, wk_ref[...]).astype(BF16)
    v = matmul(tokens, wv_ref[...]).astype(BF16)
    g = jax.nn.sigmoid(matmul(tokens, wg_ref[...]))
    gated = []
    for rr in range(2):
        lo, hi = rr * count, (rr + 1) * count
        masked = jnp.concatenate(
            [jnp.where(head_mask((count, FEATURES), h), q[lo:hi], 0.0) for h in range(HEADS)], axis=0
        ).astype(BF16)
        logits = lax.dot_general(masked, k[lo:hi], NT, preferred_element_type=F32) * SCALE
        e = jnp.exp(logits - jnp.max(logits, axis=-1, keepdims=True))
        share = 1.0 / jnp.sum(e, axis=-1, keepdims=True)
        out = matmul(e.astype(BF16), v[lo:hi]) * share
        attended = jnp.zeros((count, FEATURES), F32)
        for h in range(HEADS):
            attended = jnp.where(
                head_mask(attended.shape, h), out[h * count : (h + 1) * count], attended
            )
        gated.append((g[lo:hi] * attended).astype(BF16))
    update = tokens_of(1) + matmul(jnp.concatenate(gated, axis=0), wo_ref[...])
    for rr in range(2):
        for s in range(2):
            at = (rr * 2 + s) * CHIPS
            for half in range(2):
                u_scr[pl.ds(s * CHIPS * 4 + rr * 2 + half, CHIPS, stride=4), :] = update[
                    at : at + CHIPS, half * 128 : (half + 1) * 128
                ]
    out_ref[...] = u_scr[...].astype(BF16)


def final_kernel(x_ref, rows_ref, out_ref, t_scr):
    t_scr[...] = x_ref[...].astype(F32)
    part = [t_scr[pl.ds(s * CHIPS * 4 + i, CHIPS, stride=4), :] for s in range(2) for i in range(4)]
    step = rows_ref.shape[0] // (2 * ZH)
    for s in range(2):
        update = jnp.concatenate(
            [jnp.concatenate([part[s * 4 + rr * 2], part[s * 4 + rr * 2 + 1]], axis=1) for rr in range(2)],
            axis=0,
        )
        for z in range(ZH):
            at = (z * 2 + s) * step
            out_ref[at : at + step] = rows_ref[at : at + step] + update[z * step : (z + 1) * step]


def shards(
    alignment,
    pair,
    offset_matrix,
    row_wq,
    row_wk,
    row_wv,
    row_wg,
    row_wo,
    col_wq,
    col_wk,
    col_wv,
    col_wg,
    col_wo,
):
    core = lax.axis_index("c").astype(jnp.int32)
    core_ref = core.reshape(1)
    tokens = alignment.shape[1]
    half = tokens // 2
    swap = [(0, 1), (1, 0)]
    turn = [
        (b * BLOCKS + r, (b ^ TURN[b ^ r]) * BLOCKS + b) for b in range(BLOCKS) for r in range(BLOCKS)
    ]

    pair_shape = pair.shape
    bias_shape = (HEADS, pair_shape[0], pair_shape[1])
    bias_here = call(
        pair_kernel,
        jax.ShapeDtypeStruct(bias_shape, BF16),
        offset_matrix.T,
        pair,
        hbm=2,
        scratch=[
            pltpu.VMEM((HEADS, pair_shape[2]), F32),
            pltpu.VMEM(pair_shape, F32),
            pltpu.VMEM(bias_shape, F32),
            pltpu.SemaphoreType.DMA((3,)),
        ],
    )
    bias = lax.ppermute(bias_here, ("y", "zl", "x"), turn)
    normed = call(norm_kernel, jax.ShapeDtypeStruct((tokens, FEATURES), BF16), alignment[0])
    near_normed = lax.all_gather(normed, "zl", axis=0, tiled=True)
    near_normed, bias = lax.optimization_barrier((near_normed, bias))
    own_normed = lax.all_gather(near_normed, "x", axis=0, tiled=True)
    pair_normed = lax.ppermute(own_normed, "c", swap)
    rows = lax.all_gather(alignment, "c", axis=0, tiled=True)
    rows = rows.reshape(2, ZH, 2, half // ZH, FEATURES)

    wide = jnp.broadcast_to(bias[None], (CHIPS,) + bias.shape)
    wide = lax.all_to_all(wide, ("y", "zh"), 0, 0, tiled=True)

    here_ref = lax.axis_index(RES).astype(jnp.int32).reshape(1)
    q, g, mine = call(
        query_kernel,
        (
            jax.ShapeDtypeStruct((2, half, FEATURES), BF16),
            jax.ShapeDtypeStruct((2, half, FEATURES), F32),
            jax.ShapeDtypeStruct((2, half, FEATURES), F32),
        ),
        core_ref,
        rows,
        row_wq,
        row_wg,
        smem=1,
        flops=2 * 2 * half * FEATURES * 2 * FEATURES,
        size=2**20,
    )
    send = row_call(
        core_ref, here_ref, q, own_normed, pair_normed, row_wk, row_wv, wide, g, mine, row_wo
    )

    block = lax.all_to_all(send, ("zh", "y"), 0, 0, tiled=True)
    update = call(
        column_kernel,
        jax.ShapeDtypeStruct((CHIPS * 8, 128), BF16),
        block,
        col_wq,
        col_wk,
        col_wv,
        col_wg,
        col_wo,
        scratch=[pltpu.VMEM((CHIPS * 16, 128), F32), pltpu.VMEM((CHIPS * 8, 128), F32)],
    )
    back = lax.all_to_all(update.reshape(2 * CHIPS, 4, 128), ("c", "zh", "y"), 0, 0, tiled=True)
    out = call(
        final_kernel,
        jax.ShapeDtypeStruct((tokens, FEATURES), F32),
        back.reshape(CHIPS * 8, 128),
        alignment[0],
        scratch=[pltpu.VMEM((CHIPS * 8, 128), F32)],
    )
    return out[None]


def solution(mesh):
    fine = Mesh(mesh.devices.reshape(Y, ZH, C, ZL, X), ("y", "zh", "c", "zl", "x"))
    split = P(SEQ, RES, None)
    in_specs = (split, split) + (P(),) * 11
    return jax.shard_map(shards, mesh=fine, in_specs=in_specs, out_specs=split, check_vma=False)
```
